512 devices in a mesh: seg: 128 (over y, x, z_lo, core), det: 4 (over z_hi).
Axes of the slice: x: 4, y: 8, z: 8 (z_hi: 4, z_lo: 2; z = z_hi * 2 + z_lo), core: 2. Of those that a mesh axis runs over, the one named last changes fastest.
Arguments:
- strain: bfloat16 [4, 128, 2, 16, 128], P('det', 'seg'), may hold values from -6 to 6
- bank: bfloat16 [512, 16, 2, 16, 128], P('seg'), as said below
- bank_list: int32 [128, 6], replicated, may hold values from 0 to 511, as said below
- block_len: int32 [512], replicated, may hold values from 1 to 16, 4352 in all
- band_edges: int32 [7], replicated, may hold values from 129 to 1919, as said below
Outputs:
- net_stat: float32 [4, 128, 96, 32, 128], P('det', 'seg')
The draws below stay inside these ranges and needn't reach their ends.
Inputs may be any that keep to these rules, and one draw needn't show every extreme that they name: Each row of bank_list names 6 different blocks, all stored by the 8 owners with index s, s + 1, ..., s + 8 - 1 modulo 128 for segment s; at most 2 of them are stored by one owner, and exactly 2 by some owner in every row. `band_edges`: strictly rising; every band holds more than 128 bins. `bank`: entries independent, with scales that vary from template to template and from bin to bin.
All inputs are finite; a program needn't handle non-finite values.
Results may differ from the reference program's by a relative error of at most 0.0031.
Values may be sent and summed in bfloat16 or wider, within the bound.
A program may use at most 64 MiB of HBM per device.

```python
import math
import jax
import jax.numpy as jnp
import numpy as np
from jax import lax

KA = 128
KH = 16
NB = 8
BLKLEN = 16
BLK_DEV = 4
REACH = 8
PER_OWNER = 2
ASSIGN = 6
NF = 2048
TLEN = 4096
TB = 32
SEGS = 128
DETS = 4
NBLK = 512
SLOTS = 96


def draw_bank(key, part):
    key_base, key_tmpl, key_bins = jax.random.split(key, 3)
    shape = (NBLK, BLKLEN, 2, KH, KA)
    base = jax.random.normal(key_base, shape, jnp.float32)
    tmpl_scale = jnp.exp(jax.random.uniform(key_tmpl, (NBLK, BLKLEN, 1, 1, 1), jnp.float32, 0.0, math.log(10.0)))
    bin_scale = jnp.exp(jax.random.uniform(key_bins, (NBLK, BLKLEN, 1, KH, KA), jnp.float32, 0.0, math.log(10.0)))
    return (0.3 * base * tmpl_scale * bin_scale).astype(jnp.bfloat16)


def draw_bank_list(key, part):

    def one_list(seg_key, seg_idx):
        key_owner, key_units, key_local = jax.random.split(seg_key, 3)
        owners = jax.random.permutation(key_owner, REACH)
        units = jax.random.permutation(key_units, (REACH - 1) * PER_OWNER)[:ASSIGN - PER_OWNER]
        offsets = jnp.concatenate([jnp.full((PER_OWNER,), owners[0], jnp.int32), owners[1 + units // PER_OWNER].astype(jnp.int32)])
        ranks = jnp.concatenate([jnp.arange(PER_OWNER, dtype=jnp.int32), (units % PER_OWNER).astype(jnp.int32)])
        local_perm = jax.vmap(lambda off_idx: jax.random.permutation(jax.random.fold_in(key_local, off_idx), BLK_DEV))(jnp.arange(REACH, dtype=jnp.int32))
        local_id = local_perm[offsets, ranks].astype(jnp.int32)
        owner_seg = (seg_idx + offsets) % SEGS
        return owner_seg * BLK_DEV + local_id
    seg_keys = jax.random.split(key, SEGS)
    return jax.vmap(one_list)(seg_keys, jnp.arange(SEGS, dtype=jnp.int32)).astype(jnp.int32)


def draw_band_edges(key, part):
    cuts = jax.random.permutation(key, NF // 2 - 2)[:NB - 2] + 1
    ordered = jnp.concatenate([jnp.sort(cuts).astype(jnp.int32), jnp.full((1,), NF // 2 - 1, jnp.int32)])
    return (ordered + jnp.arange(1, NB, dtype=jnp.int32) * (NF // (2 * NB))).astype(jnp.int32)


def steps_of(rng, shape, cuts, low, largest):
    gain = 1.0
    for axis_at, shards_of in cuts:
        draws = jax.random.uniform(jax.random.fold_in(jax.random.fold_in(rng, 6), axis_at), (shards_of,), jnp.float32, low / len(cuts), largest / len(cuts))
        gain = gain * jnp.repeat(jnp.exp(draws), shape[axis_at] // shards_of).reshape((-1,) + (1,) * (len(shape) - 1 - axis_at))
    return gain


def profile(number_of, total, limit, skew):
    loads = [(1 << 20) // math.isqrt(grade ** skew) + 1 for grade in range(2, number_of + 1)]
    surplus, given = total - limit - (number_of - 1), [1] * (number_of - 1)
    while surplus > 0:
        candidates = [i for i in range(number_of - 1) if given[i] < limit]
        whole, left = sum([loads[i] for i in candidates]), surplus
        for i in candidates:
            more = min(limit - given[i], max(1, left * loads[i] // whole), surplus)
            given[i] = given[i] + more
            surplus = surplus - more
    return np.array([limit] + given)


def ragged_sizes(key, count, total, bound, skew):
    if count == 2:
        one = jax.random.randint(key, (), max(1, total - bound), min(bound, total - 1) + 1)
        return jnp.stack([one, total - one])
    sizes = jnp.asarray(profile(count, total, bound, skew), jnp.int32)
    couples = (count - 1) // 2
    source_of, sink = sizes[1:1 + 2 * couples:2], sizes[2:2 + 2 * couples:2]
    room = jnp.minimum(source_of - 1, bound - sink)
    shifted = jax.random.randint(jax.random.fold_in(key, 1), (couples,), 0, 1 << 20) % (room + 1)
    sizes = sizes.at[1:1 + 2 * couples:2].set(source_of - shifted).at[2:2 + 2 * couples:2].set(sink + shifted)
    return sizes[jax.random.permutation(jax.random.fold_in(key, 2), count)]


def scatter_about(own_key, dims, scale, bound, cuts=(), kind=jnp.bfloat16):
    values = scale * jax.random.normal(own_key, dims, jnp.float32)
    if cuts:
        values = values * steps_of(own_key, dims, cuts, -0.22, 0.18)
    return jnp.clip(values, -bound, bound).astype(kind)


def setup_inputs(seed: int = 0) -> dict:
    key_of = jax.random.split(jax.random.key(seed), 6)
    return {
        "strain": scatter_about(key_of[0], (DETS, SEGS, 2, KH, KA), 1.0, 6.0, ((0, 4), (1, 128))),
        "bank": draw_bank(jax.random.fold_in(key_of[5], 71), 0),
        "bank_list": draw_bank_list(jax.random.fold_in(key_of[5], 71), 0),
        "block_len": ragged_sizes(key_of[3], NBLK, NBLK * (BLKLEN + 1) // 2, BLKLEN, 0).astype(jnp.int32),
        "band_edges": draw_band_edges(jax.random.fold_in(key_of[5], 71), 0),
    }


epsilon = 1e-06
highest = lax.Precision.HIGHEST

def reference(strain, bank, bank_list, block_len, band_edges):
    bin_index = jnp.arange(NF, dtype=jnp.int32)
    band_of = lax.optimization_barrier(jnp.sum((bin_index[:, None] >= band_edges[None, :]).astype(jnp.int32), axis=1))
    band_mask = (band_of[None, :] == jnp.arange(NB, dtype=jnp.int32)[:, None]).astype(jnp.float32)
    partner_of = jnp.bitwise_xor(jnp.arange(DETS, dtype=jnp.int32), 2)

    def one_segment(seg_idx):
        block_ids = bank_list[seg_idx]
        templates = bank[block_ids].reshape(SLOTS, 2, NF).astype(jnp.float32)
        live_mask = (jnp.arange(BLKLEN, dtype=jnp.int32)[None, :] < block_len[block_ids][:, None]).astype(jnp.float32).reshape(SLOTS)
        strain_spec = lax.dynamic_index_in_dim(strain, seg_idx, 1, keepdims=False).reshape(DETS, 2, NF).astype(jnp.float32)
        tmpl_re = templates[:, 0]
        tmpl_im = templates[:, 1]
        tmpl_power = tmpl_re * tmpl_re + tmpl_im * tmpl_im
        band_power = jnp.dot(tmpl_power, band_mask.T, precision=highest) + epsilon
        total_power = lax.optimization_barrier(jnp.sum(band_power, axis=1))
        band_share = band_power / total_power[:, None]
        inv_norm = 1.0 / jnp.sqrt(total_power)

        def one_det(det_data):
            cross_re = det_data[0] * tmpl_re + det_data[1] * tmpl_im
            cross_im = det_data[1] * tmpl_re - det_data[0] * tmpl_im
            cross_spec = (cross_re + 1j * cross_im)[:, None, :] * band_mask[None]
            padded = jnp.concatenate([cross_spec, jnp.zeros_like(cross_spec)], axis=-1)
            band_snr = jnp.fft.ifft(padded, axis=-1) * TLEN * inv_norm[:, None, None]
            total_snr = lax.optimization_barrier(jnp.sum(band_snr, axis=1))
            residue = band_snr - band_share[:, :, None] * total_snr[:, None]
            chi_square = lax.optimization_barrier(jnp.sum((residue.real * residue.real + residue.imag * residue.imag) / band_share[:, :, None], axis=1))
            snr_rows = jnp.stack([total_snr.real, total_snr.imag], axis=1)
            return (snr_rows, chi_square)
        snr_rows, chi_square = lax.map(one_det, strain_spec)
        rounded = lax.optimization_barrier(snr_rows.astype(jnp.bfloat16)).astype(jnp.float32)
        partner = rounded[partner_of]
        joined = snr_rows + partner
        coherent = 0.5 * lax.optimization_barrier(jnp.sum(joined * joined, axis=2))
        statistic = coherent / (1.0 + chi_square / (2.0 * (NB - 1))) * live_mask[None, :, None]
        return jnp.swapaxes(statistic.reshape(DETS, SLOTS, KA, TB), 2, 3)
    result = lax.map(one_segment, jnp.arange(SEGS, dtype=jnp.int32))
    return jnp.swapaxes(result, 0, 1)
```

```python
import functools

import jax
import jax.numpy as jnp
import numpy as np
from jax import lax
from jax.experimental import pallas as pl
from jax.experimental.pallas import tpu as pltpu
from jax.sharding import PartitionSpec as P

MESH = pl.DeviceIdType.MESH
EPS = 1e-06
ONE_SCALE = 1.62445
TWO_SCALE = 1.62475
BANDS = 8
ROWS = 592
REACH = 8
UNIT = 4


def tables():
    first = np.zeros((ROWS, 256))
    turn = 2 * np.pi * np.outer(np.arange(32), np.arange(16)) / 32
    cos, sin = np.cos(turn), np.sin(turn)
    from_re, from_im = (cos, sin), (-sin, cos)
    for out_part in range(2):
        both = np.concatenate([from_re[out_part], from_im[out_part]], axis=1)
        for band in range(BANDS):
            at = out_part * 256 + band * 32
            first[at : at + 32, :128] = np.tile(both, (1, 4))
        at = 512 + out_part * 32
        first[at : at + 32, 128:192] = np.tile(both, (1, 2))
    first *= ONE_SCALE
    first[576:584, 192:] = 1.0
    turn = 2 * np.pi * np.outer(np.arange(32), np.arange(128)) / 4096
    twist = np.stack([np.cos(turn), np.sin(turn)]) / (ONE_SCALE * TWO_SCALE)
    turn = 2 * np.pi * (np.outer(np.arange(128), np.arange(128)) % 128) / 128
    cos, sin = np.cos(turn), np.sin(turn)
    second = TWO_SCALE * np.block([[cos, sin], [-sin, cos]])
    return (
        jnp.asarray(first, jnp.bfloat16),
        jnp.asarray(twist, jnp.float32),
        jnp.asarray(second, jnp.bfloat16),
    )


def move_kernel(bank, strain, held, partner, send_sem, recv_sem, own_sem, strain_sem):
    chunks = bank.shape[0]
    segs = lax.axis_size("seg")
    dets = lax.axis_size("det")
    seg = lax.axis_index("seg")
    det = lax.axis_index("det")
    core = lax.rem(seg, 2)
    low = lax.rem(lax.div(seg, 2), 2)
    part = 2 * low + core
    peer = seg + 1 - 2 * core
    across = seg + 2 - 4 * low

    def wrapped(index):
        return lax.rem(index + segs, segs)

    next_det = lax.rem(det + 1, dets)
    prev_det = lax.rem(det + dets - 1, dets)
    other = lax.rem(det + 2, dets) if dets == 4 else det
    barrier = pltpu.get_barrier_semaphore()

    def greet(to_seg, to_det):
        pl.semaphore_signal(barrier, inc=1, device_id=(to_seg, to_det), device_id_type=MESH)

    greet(wrapped(seg + 4), det)
    greet(peer, det)
    greet(across, det)
    greet(seg, other)

    @pl.when(low == 0)
    def _():
        greet(seg + 2, prev_det)

    @pl.when(core == 1)
    def _():
        greet(wrapped(seg + 3), det)

    @pl.when(part == 2)
    def _():
        greet(wrapped(seg + 5), det)

    pl.semaphore_wait(barrier, 4 + low + (1 - core) + jnp.where(part == 3, 1, 0))

    def copy(kind, source, k, slot, to_seg, to_det):
        return pltpu.make_async_remote_copy(
            src_ref=source,
            dst_ref=held.at[slot, k],
            send_sem=send_sem.at[kind, k],
            recv_sem=recv_sem.at[slot, k],
            device_id=(to_seg, to_det),
            device_id_type=MESH,
        )

    def own_along(k):
        return copy(0, bank.at[k], k, 4, wrapped(seg - 4), det)

    def own_peer(k):
        return copy(1, bank.at[k], k, 1, peer, det)

    def own_across(k):
        return copy(2, bank.at[k], k, 2, seg - 2, next_det)

    def pass_two(k):
        return copy(1, held.at[2, k], k, 1 + 2 * core, peer, det)

    def pass_four_peer(k):
        return copy(3, held.at[4, k], k, 3 + 2 * core, peer, det)

    def pass_four_across(k):
        return copy(4, held.at[4, k], k, 2 + 4 * low, across, det)

    def pass_four_along(k):
        return copy(5, held.at[4, k], k, 7, wrapped(seg - 3), det)

    slot_across = 6 - 4 * low

    def pass_across_peer(k):
        return copy(6, held.at[slot_across, k], k, slot_across - 1 + 2 * core, peer, det)

    def pass_across_along(k):
        return copy(5, held.at[2, k], k, 7, wrapped(seg - 5), det)

    def relay_one(k):
        return copy(7, held.at[7, k], k, 5, seg + 2, det)

    def relay_two(k):
        return copy(7, held.at[7, k], k, 6, peer, det)

    def relay_three(k):
        return copy(7, held.at[5, k], k, 6, peer, det)

    def arrived(slot, k):
        pltpu.make_async_copy(held.at[slot, k], held.at[slot, k], recv_sem.at[slot, k]).wait()

    exchange = pltpu.make_async_remote_copy(
        src_ref=strain.at[0, 0],
        dst_ref=partner,
        send_sem=strain_sem.at[0],
        recv_sem=strain_sem.at[1],
        device_id=(seg, other),
        device_id_type=MESH,
    )
    stay = pltpu.make_async_copy(bank, held.at[0], own_sem)
    for k in range(chunks):
        own_along(k).start()

        @pl.when(low == 1)
        def _():
            own_across(k).start()

    for k in range(chunks):

        @pl.when(core == 1)
        def _():
            own_peer(k).start()

    exchange.start()
    stay.start()
    for step in range(chunks + 3):
        k = step
        if k < chunks:
            arrived(4, k)

            @pl.when(core == 0)
            def _():
                pass_four_along(k).start()

            pass_four_across(k).start()
            pass_four_peer(k).start()
        k = step - 1
        if 0 <= k < chunks:
            arrived(slot_across, k)

            @pl.when(part == 3)
            def _():
                pass_across_along(k).start()

            pass_across_peer(k).start()

            @pl.when(low == 0)
            def _():
                arrived(2, k)

            @pl.when(part == 0)
            def _():
                pass_two(k).start()

            @pl.when(part == 1)
            def _():
                own_peer(k).wait_send()
                pass_two(k).start()

        k = step - 2
        if 0 <= k < chunks:

            @pl.when(part == 1)
            def _():
                arrived(7, k)
                relay_one(k).start()

            @pl.when(part == 2)
            def _():
                arrived(7, k)
                relay_two(k).start()

        k = step - 3
        if 0 <= k < chunks:

            @pl.when(part == 3)
            def _():
                arrived(5, k)
                relay_three(k).start()

    for k in range(chunks):
        arrived(1, k)
        arrived(3, k)

        @pl.when(part != 3)
        def _():
            arrived(5, k)

        @pl.when(low == 1)
        def _():
            arrived(6, k)

        @pl.when((part == 0) | (part == 3))
        def _():
            arrived(7, k)

        own_along(k).wait_send()

        @pl.when(low == 1)
        def _():
            own_across(k).wait_send()

        @pl.when((low == 0) | (core == 1))
        def _():
            own_peer(k).wait_send()

        pass_four_peer(k).wait_send()
        pass_four_across(k).wait_send()

        @pl.when((core == 0) | (part == 3))
        def _():
            pass_four_along(k).wait_send()

        pass_across_peer(k).wait_send()

        @pl.when(part != 0)
        def _():
            relay_one(k).wait_send()

    exchange.wait()
    stay.wait()


def move(bank, strain):
    return pl.pallas_call(
        move_kernel,
        out_shape=(
            jax.ShapeDtypeStruct((REACH,) + bank.shape, bank.dtype),
            jax.ShapeDtypeStruct(strain.shape[2:], strain.dtype),
        ),
        in_specs=[pl.BlockSpec(memory_space=pl.ANY)] * 2,
        out_specs=(pl.BlockSpec(memory_space=pl.ANY),) * 2,
        scratch_shapes=[
            pltpu.SemaphoreType.DMA((8, bank.shape[0])),
            pltpu.SemaphoreType.DMA((REACH, bank.shape[0])),
            pltpu.SemaphoreType.DMA,
            pltpu.SemaphoreType.DMA((2,)),
        ],
        compiler_params=pltpu.CompilerParams(
            collective_id=0, has_side_effects=True
        ),
        name="move",
    )(bank, strain)


def band_at(bins, edges):
    return sum(jnp.where(bins >= edges[e], 1, 0) for e in range(BANDS - 1))


def filter_kernel(
    held, strain, partner, bank_list, block_len, edges, first, twist, second, out,
    blocks, banded, cross, stage, turned, result, order, block_sem, out_sem,
):
    segs = lax.axis_size("seg")
    seg = lax.axis_index("seg")
    assign = blocks.shape[0]
    owned = held.shape[1]
    width = blocks.shape[1]
    slots = assign * width

    def fetch(q):
        block = bank_list[q, seg]
        owner = lax.div(block, owned)
        offset = lax.rem(owner - seg + segs, segs)
        return pltpu.make_async_copy(
            held.at[offset, lax.rem(block, owned)], blocks.at[q], block_sem.at[q]
        )

    def give(q):
        rows = pl.ds(q * width, width)
        return pltpu.make_async_copy(result.at[rows], out.at[0, 0, rows], out_sem.at[q])

    for q in range(assign):
        fetch(q).start()

    ends = []
    end = 0
    for q in range(assign):
        live = block_len[bank_list[q, seg]]

        @pl.loop(0, live)
        def _(m, q=q, start=end):
            order[start + m] = q * width + m

        end = end + live
        ends.append(end)

        @pl.loop(live, width)
        def _(m, q=q):
            result[q * width + m] = jnp.zeros(result.shape[1:], jnp.float32)

    for m in range(2 * UNIT):
        order[end + m] = slots

    row = lax.broadcasted_iota(jnp.int32, (ROWS, 256), 0)
    lane = lax.broadcasted_iota(jnp.int32, (1, 256), 1)
    high_lane = jnp.where(lane < 128, lax.rem(lax.div(lane, 32), 2), lax.rem(lax.div(lane, 16), 2))
    lane_band = band_at(lax.rem(lane, 16) * 128 + 127 * high_lane, edges)
    row_band = jnp.where(row < 512, lax.rem(lax.div(row, 32), BANDS), row - 576)
    keep = ((row >= 512) & (row < 576)) | (row_band == lane_band)
    banded[...] = jnp.where(keep, first[...].astype(jnp.float32), 0.0).astype(jnp.bfloat16)

    bins = lax.broadcasted_iota(jnp.int32, (16, 128), 0) * 128
    at_low = band_at(bins, edges)
    at_own = band_at(bins + lax.broadcasted_iota(jnp.int32, (16, 128), 1), edges)
    low_mask = jnp.where(at_low == at_own, 1.0, 0.0)
    high_mask = (1.0 - low_mask).astype(jnp.bfloat16)
    low_mask = low_mask.astype(jnp.bfloat16)

    data_re = strain[0, 0, 0].astype(jnp.float32)
    data_im = strain[0, 0, 1].astype(jnp.float32)
    other_re = partner[0].astype(jnp.float32)
    other_im = partner[1].astype(jnp.float32)

    def halves(value):
        top = value.astype(jnp.bfloat16)
        return top, (value - top.astype(jnp.float32)).astype(jnp.bfloat16)

    def products(unit, h):
        for t in range(2):
            lanes = slice(t * 128, t * 128 + 128)
            slot = order[unit * UNIT + 2 * h + t]
            slot = jnp.where(slot == slots, 0, slot)
            q, m = lax.div(slot, width), lax.rem(slot, width)
            tmpl_re = blocks[q, m, 0].astype(jnp.float32)
            tmpl_im = blocks[q, m, 1].astype(jnp.float32)

            def put(at, value):
                cross[h, at : at + 16, lanes] = value

            for at, value in (
                (0, data_re * tmpl_re + data_im * tmpl_im),
                (16, data_im * tmpl_re - data_re * tmpl_im),
            ):
                top, rest = halves(value)
                put(at, top * low_mask)
                put(at + 32, top * high_mask)
                put(at + 64, rest * low_mask)
                put(at + 96, rest * high_mask)
            for at, value in (
                (128, other_re * tmpl_re + other_im * tmpl_im),
                (144, other_im * tmpl_re - other_re * tmpl_im),
            ):
                top, rest = halves(value)
                put(at, top)
                put(at + 32, rest)
            top, rest = halves(tmpl_re * tmpl_re + tmpl_im * tmpl_im)
            put(192, top * low_mask)
            put(208, top * high_mask)
            put(224, rest * low_mask)
            put(240, rest * high_mask)
        stage[h] = jnp.dot(banded[...], cross[h], preferred_element_type=jnp.float32)

    def turn(h):
        cos, sin = twist[0], twist[1]
        for t in range(2):
            lanes = slice(t * 128, t * 128 + 128)
            for band in range(BANDS + 1):
                at = 512 if band == BANDS else 32 * band
                gap = 32 if band == BANDS else 256
                part_re = stage[h, at : at + 32, lanes]
                part_im = stage[h, at + gap : at + gap + 32, lanes]
                rows = slice(32 * band, 32 * band + 32)
                turned[h, t, rows, :128] = (part_re * cos - part_im * sin).astype(jnp.bfloat16)
                turned[h, t, rows, 128:] = (part_re * sin + part_im * cos).astype(jnp.bfloat16)

    def finish(unit, h, powers):
        for t in range(2):
            power = powers[t]
            total = jnp.sum(power, axis=0, keepdims=True)
            weight = 1.0 / power
            series = jnp.dot(turned[h, t], second[...], preferred_element_type=jnp.float32)
            norm = lax.rsqrt(total)
            sum_re = sum_im = spread = 0.0
            for band in range(BANDS):
                band_re = series[32 * band : 32 * band + 32, :128]
                band_im = series[32 * band : 32 * band + 32, 128:]
                sum_re = sum_re + band_re
                sum_im = sum_im + band_im
                spread = spread + (band_re * band_re + band_im * band_im) * weight[band : band + 1]
            snr_re = sum_re * norm
            snr_im = sum_im * norm
            chi_square = spread - (snr_re * snr_re + snr_im * snr_im)
            join_re = snr_re + series[256:, :128] * norm
            join_im = snr_im + series[256:, 128:] * norm
            coherent = 0.5 * (join_re * join_re + join_im * join_im)
            chi_square = jnp.maximum(chi_square, 0.0)
            result[order[unit * UNIT + 2 * h + t]] = coherent / (
                1.0 + chi_square * (1.0 / (2 * (BANDS - 1)))
            )

    for q in range(assign):
        fetch(q).wait()
    for h in range(UNIT // 2):
        products(0, h)
    done = 0
    for q in range(assign):
        last = q == assign - 1
        upto = lax.div(ends[q] + (UNIT - 1 if last else 0), UNIT)

        @pl.loop(done, upto)
        def _(unit):
            powers = []
            for h in range(UNIT // 2):
                turn(h)
                powers.append(
                    [
                        jnp.sum(stage[h, 576:584, t * 128 : t * 128 + 128], axis=1, keepdims=True) + EPS
                        for t in range(2)
                    ]
                )
            for h in range(UNIT // 2):
                finish(unit, h, powers[h])
                products(unit + 1, h)

        for g in range(q + 1):

            @pl.when((ends[g] <= UNIT * upto) & (ends[g] > UNIT * done) if not last else ends[g] > UNIT * done)
            def _(g=g):
                give(g).start()

        done = upto

    for q in range(assign):
        give(q).wait()


def correlate(held, strain, partner, bank_list, block_len, edges):
    _, owned, width, _, half_rows, bins = held.shape
    assign = bank_list.shape[1]
    slots = assign * width
    vmem = pl.BlockSpec(memory_space=pltpu.VMEM)
    smem = pl.BlockSpec(memory_space=pltpu.SMEM)
    hbm = pl.BlockSpec(memory_space=pl.ANY)
    return pl.pallas_call(
        filter_kernel,
        out_shape=jax.ShapeDtypeStruct((1, 1, slots, 2 * half_rows, bins), jnp.float32),
        in_specs=[hbm, vmem, vmem, smem, smem, smem, vmem, vmem, vmem],
        out_specs=hbm,
        scratch_shapes=[
            pltpu.VMEM((assign,) + held.shape[2:], held.dtype),
            pltpu.VMEM((ROWS, 256), jnp.bfloat16),
            pltpu.VMEM((UNIT // 2, 256, 256), jnp.bfloat16),
            pltpu.VMEM((UNIT // 2, ROWS, 256), jnp.float32),
            pltpu.VMEM((UNIT // 2, 2, 288, 256), jnp.bfloat16),
            pltpu.VMEM((slots + 1, 2 * half_rows, bins), jnp.float32),
            pltpu.SMEM((slots + 2 * UNIT,), jnp.int32),
            pltpu.SemaphoreType.DMA((assign,)),
            pltpu.SemaphoreType.DMA((assign,)),
        ],
        compiler_params=pltpu.CompilerParams(vmem_limit_bytes=60 * 2**20),
        name="filter",
    )(held, strain, partner, bank_list.T, block_len, edges, *tables())


def body(strain, bank, bank_list, block_len, band_edges):
    held, partner = move(bank, strain)
    return correlate(held, strain, partner, bank_list, block_len, band_edges)


def solution(mesh):
    return jax.shard_map(
        body,
        mesh=mesh,
        in_specs=(
            P("det", "seg", None, None, None),
            P("seg", None, None, None, None),
            P(),
            P(),
            P(),
        ),
        out_specs=P("det", "seg", None, None, None),
        check_vma=False,
    )
```

```python
import functools

import jax
import jax.numpy as jnp
import numpy as np
from jax import lax
from jax.experimental import pallas as pl
from jax.experimental.pallas import tpu as pltpu
from jax.sharding import PartitionSpec as P

MESH = pl.DeviceIdType.MESH
EPS = 1e-06
ONE_SCALE = 1.62445
TWO_SCALE = 1.62475
BANDS = 8
ROWS = 592
REACH = 8
ALONG = 4
CHUNKS = 4
UNIT = 4


def tables():
    first = np.zeros((ROWS, 256))
    turn = 2 * np.pi * np.outer(np.arange(32), np.arange(16)) / 32
    cos, sin = np.cos(turn), np.sin(turn)
    from_re, from_im = (cos, sin), (-sin, cos)
    for out_part in range(2):
        both = np.concatenate([from_re[out_part], from_im[out_part]], axis=1)
        for band in range(BANDS):
            at = out_part * 256 + band * 32
            first[at : at + 32, :128] = np.tile(both, (1, 4))
        at = 512 + out_part * 32
        first[at : at + 32, 128:192] = np.tile(both, (1, 2))
    first *= ONE_SCALE
    first[576:584, 192:] = 1.0
    turn = 2 * np.pi * np.outer(np.arange(32), np.arange(128)) / 4096
    twist = np.stack([np.cos(turn), np.sin(turn)]) / (ONE_SCALE * TWO_SCALE)
    turn = 2 * np.pi * (np.outer(np.arange(128), np.arange(128)) % 128) / 128
    cos, sin = np.cos(turn), np.sin(turn)
    second = TWO_SCALE * np.block([[cos, sin], [-sin, cos]])
    return (
        jnp.asarray(first, jnp.bfloat16),
        jnp.asarray(twist, jnp.float32),
        jnp.asarray(second, jnp.bfloat16),
    )


def move_kernel(
    bank, strain, held, passing, partner, line, send_sem, recv_sem, pass_sem, own_sem, line_sem
):
    chunks = bank.shape[0]
    half = chunks // 2
    segs = lax.axis_size("seg")
    dets = lax.axis_size("det")
    seg = lax.axis_index("seg")
    det = lax.axis_index("det")
    core = lax.rem(seg, 2)
    low = lax.rem(lax.div(seg, 2), 2)
    part = 2 * low + core
    peer = seg + 1 - 2 * core
    across = seg + 2 - 4 * low
    last = dets - 1
    around = 4 * ALONG

    def wrapped(index):
        return lax.rem(index + segs, segs)

    def beside(index, by):
        return lax.div(index, around) * around + lax.rem(index + by + around, around)

    above = beside(seg, 4)
    below = beside(seg, -4)
    next_det = lax.rem(det + 1, dets)
    prev_det = lax.rem(det + dets - 1, dets)
    barrier = pltpu.get_barrier_semaphore()

    def greet(to_seg, to_det):
        pl.semaphore_signal(barrier, inc=1, device_id=(to_seg, to_det), device_id_type=MESH)

    greet(wrapped(seg + 4), det)
    greet(peer, det)
    greet(across, det)

    @pl.when(low == 0)
    def _():
        greet(across, prev_det)

    @pl.when((low == 1) & (det < last))
    def _():
        greet(across, det + 1)

    @pl.when(core == 0)
    def _():
        greet(below, det)

    @pl.when(core == 1)
    def _():
        greet(beside(wrapped(seg + 7), 4), det)

    @pl.when(part == 2)
    def _():
        greet(wrapped(seg + 3), det)
        greet(wrapped(seg + 5), det)

    pl.semaphore_wait(barrier, 5 - core + jnp.where((low == 1) | (det > 0), 1, 0))

    def copy(kind, source, k, slot, to_seg, to_det):
        return pltpu.make_async_remote_copy(
            src_ref=source,
            dst_ref=held.at[slot, k],
            send_sem=send_sem.at[kind],
            recv_sem=recv_sem.at[slot, jnp.where((slot == 1) | (slot == 3), 0, k)],
            device_id=(to_seg, to_det),
            device_id_type=MESH,
        )

    def arrived(slot, k):
        pltpu.make_async_copy(held.at[slot, k], held.at[slot, k], recv_sem.at[slot, k]).wait()

    def all_arrived(slot):
        pltpu.make_async_copy(held.at[slot], held.at[slot], recv_sem.at[slot, 0]).wait()

    def sent(kind, count):
        some = bank.at[pl.ds(0, count)]
        pltpu.make_async_copy(some, some, send_sem.at[kind]).wait()

    def up_across(kind, source, k, slot):
        if k % 2 == 0:
            copy(kind, source, k, slot, seg + 2, det).start()
        else:

            @pl.when(det > 0)
            def _():
                copy(kind, source, k, slot, seg + 2, det - 1).start()

            @pl.when(det == last)
            def _():
                copy(kind, source, k, slot, seg + 2, det).start()

    def sent_up_across(kind):
        sent(kind, half)

        @pl.when(det > 0)
        def _():
            sent(kind, half)

        @pl.when(det == last)
        def _():
            sent(kind, half)

    def own_along(k):
        copy(0, bank.at[k], k, 4, wrapped(seg - 4), det).start()

    def own_peer(k):
        copy(1, bank.at[k], k, 1, peer, det).start()

    def own_across(k):
        if k % 2 == 0:

            @pl.when(det < last)
            def _():
                copy(2, bank.at[k], k, 2, seg - 2, det + 1).start()

            @pl.when(det == 0)
            def _():
                copy(2, bank.at[k], k, 2, seg - 2, det).start()
        else:
            copy(2, bank.at[k], k, 2, seg - 2, next_det).start()

    def own_above(k):
        pltpu.make_async_remote_copy(
            src_ref=bank.at[k],
            dst_ref=passing.at[k],
            send_sem=send_sem.at[3],
            recv_sem=pass_sem.at[k],
            device_id=(above, det),
            device_id_type=MESH,
        ).start()

    def pass_above(k):
        pltpu.make_async_copy(passing.at[k], passing.at[k], pass_sem.at[k]).wait()
        copy(4, passing.at[k], k, 7, wrapped(below - 7), det).start()

    def pass_two(k):
        copy(5, held.at[2, k], k, 1 + 2 * core, peer, det).start()

    def pass_four_peer(k):
        copy(6, held.at[4, k], k, 3 + 2 * core, peer, det).start()

    def pass_four_across(k):
        @pl.when(low == 0)
        def _():
            up_across(7, held.at[4, k], k, 2)

        @pl.when(low == 1)
        def _():
            copy(7, held.at[4, k], k, 6, seg - 2, det).start()

    slot_across = 6 - 4 * low

    def pass_across_peer(k):
        copy(8, held.at[slot_across, k], k, slot_across - 1 + 2 * core, peer, det).start()

    stay = pltpu.make_async_copy(bank, held.at[0], own_sem)
    height = 2 * det + low
    hops = dets

    def along_line(way, hop):
        if way == 0:
            to_det = det + low
        else:
            to_det = det - 1 + low
        return pltpu.make_async_remote_copy(
            src_ref=strain.at[0, 0] if hop == 0 else line.at[way, hop - 1],
            dst_ref=partner if hop == hops - 1 else line.at[way, hop],
            send_sem=line_sem.at[0, way, hop],
            recv_sem=line_sem.at[1, way, hop],
            device_id=(across, to_det),
            device_id_type=MESH,
        )

    def on_line(way, hop):
        origin = height - hop if way == 0 else height + hop
        return (origin >= way * hops) & (origin < way * hops + hops)

    def pass_line(hop):
        for way in range(2):

            @pl.when(on_line(way, hop))
            def _(way=way):
                if hop > 0:
                    along_line(way, hop - 1).wait_recv()
                if hop < hops:
                    along_line(way, hop).start()

    for k in range(chunks):
        own_along(k)

        @pl.when(core == 0)
        def _():
            own_above(k)

        @pl.when(low == 1)
        def _():
            own_across(k)

    @pl.when(core == 1)
    def _():
        for k in range(chunks):
            own_peer(k)

    pass_line(0)
    stay.start()
    for step in range(chunks + 3):
        k = step
        if k < chunks:

            @pl.when(core == 0)
            def _():
                pass_above(k)

            arrived(4, k)
            if k % 2 == 0:

                @pl.when(part == 1)
                def _():
                    copy(9, held.at[4, k], k, 7, wrapped(seg - 3), det).start()

            pass_four_across(k)
            pass_four_peer(k)
        if 1 <= step <= hops:
            pass_line(step)
        k = step - 1
        if 0 <= k < chunks:
            arrived(slot_across, k)
            if k % 2 == 1:

                @pl.when(part == 3)
                def _():
                    copy(9, held.at[2, k], k, 7, wrapped(seg - 5), det).start()

            pass_across_peer(k)

            @pl.when(low == 0)
            def _():
                arrived(2, k)
                pass_two(k)

        k = step - 2
        if 0 <= k < chunks:

            @pl.when(part == 1)
            def _():
                arrived(7, k)
                up_across(10, held.at[7, k], k, 5)

            @pl.when(part == 2)
            def _():
                arrived(7, k)
                copy(10, held.at[7, k], k, 6, peer, det).start()

        k = step - 3
        if 0 <= k < chunks:

            @pl.when(part == 3)
            def _():
                arrived(5, k)
                copy(10, held.at[5, k], k, 6, peer, det).start()

    for hop in range(hops):
        for way in range(2):

            @pl.when(on_line(way, hop))
            def _(way=way, hop=hop):
                along_line(way, hop).wait_send()

    sent(0, chunks)
    sent(6, chunks)
    sent(8, chunks)

    @pl.when(core == 0)
    def _():
        sent(3, chunks)
        sent(4, chunks)

    @pl.when(core == 1)
    def _():
        sent(1, chunks)
        sent(9, half)

    @pl.when(low == 0)
    def _():
        sent(5, chunks)
        sent_up_across(7)

    @pl.when(low == 1)
    def _():
        sent(7, chunks)
        sent(2, half)
        sent(10, chunks)

        @pl.when(det < last)
        def _():
            sent(2, half)

        @pl.when(det == 0)
        def _():
            sent(2, half)

    @pl.when(part == 1)
    def _():
        sent_up_across(10)

    all_arrived(1)
    all_arrived(3)
    for k in range(chunks):

        @pl.when(part != 3)
        def _():
            arrived(5, k)

        @pl.when(low == 1)
        def _():
            arrived(6, k)

        @pl.when((part == 0) | (part == 3))
        def _():
            arrived(7, k)

    stay.wait()


def move(bank, strain, dets):
    owned, width = bank.shape[:2]
    spectrum = strain.shape[2:]
    bank = bank.reshape((CHUNKS, owned * width // CHUNKS) + bank.shape[2:])
    held, _, partner, _ = pl.pallas_call(
        move_kernel,
        out_shape=(
            jax.ShapeDtypeStruct((REACH,) + bank.shape, bank.dtype),
            jax.ShapeDtypeStruct(bank.shape, bank.dtype),
            jax.ShapeDtypeStruct(spectrum, strain.dtype),
            jax.ShapeDtypeStruct((2, dets - 1) + spectrum, strain.dtype),
        ),
        in_specs=[pl.BlockSpec(memory_space=pl.ANY)] * 2,
        out_specs=(pl.BlockSpec(memory_space=pl.ANY),) * 4,
        scratch_shapes=[
            pltpu.SemaphoreType.DMA((11,)),
            pltpu.SemaphoreType.DMA((REACH, CHUNKS)),
            pltpu.SemaphoreType.DMA((CHUNKS,)),
            pltpu.SemaphoreType.DMA,
            pltpu.SemaphoreType.DMA((2, 2, dets)),
        ],
        compiler_params=pltpu.CompilerParams(collective_id=0, has_side_effects=True),
        name="move",
    )(bank, strain)
    return held.reshape((REACH, owned, width) + bank.shape[2:]), partner


def band_at(bins, edges):
    return sum(jnp.where(bins >= edges[e], 1, 0) for e in range(BANDS - 1))


def filter_kernel(
    held, strain, partner, bank_list, block_len, edges, first, twist, second, out,
    blocks, banded, cross, stage, turned, result, order, block_sem, out_sem,
):
    segs = lax.axis_size("seg")
    seg = lax.axis_index("seg")
    assign = blocks.shape[0]
    owned = held.shape[1]
    width = blocks.shape[1]
    slots = assign * width

    def fetch(q):
        block = bank_list[q, seg]
        owner = lax.div(block, owned)
        offset = lax.rem(owner - seg + segs, segs)
        return pltpu.make_async_copy(
            held.at[offset, lax.rem(block, owned)], blocks.at[q], block_sem.at[q]
        )

    def give(q):
        rows = pl.ds(q * width, width)
        return pltpu.make_async_copy(result.at[rows], out.at[0, 0, rows], out_sem.at[q])

    for q in range(assign):
        fetch(q).start()

    ends = []
    end = 0
    for q in range(assign):
        live = block_len[bank_list[q, seg]]

        @pl.loop(0, live)
        def _(m, q=q, start=end):
            order[start + m] = q * width + m

        end = end + live
        ends.append(end)

        @pl.loop(live, width)
        def _(m, q=q):
            result[q * width + m] = jnp.zeros(result.shape[1:], jnp.float32)

    for m in range(2 * UNIT):
        order[end + m] = slots

    row = lax.broadcasted_iota(jnp.int32, (ROWS, 256), 0)
    lane = lax.broadcasted_iota(jnp.int32, (1, 256), 1)
    high_lane = jnp.where(lane < 128, lax.rem(lax.div(lane, 32), 2), lax.rem(lax.div(lane, 16), 2))
    lane_band = band_at(lax.rem(lane, 16) * 128 + 127 * high_lane, edges)
    row_band = jnp.where(row < 512, lax.rem(lax.div(row, 32), BANDS), row - 576)
    keep = ((row >= 512) & (row < 576)) | (row_band == lane_band)
    banded[...] = jnp.where(keep, first[...].astype(jnp.float32), 0.0).astype(jnp.bfloat16)

    bins = lax.broadcasted_iota(jnp.int32, (16, 128), 0) * 128
    at_low = band_at(bins, edges)
    at_own = band_at(bins + lax.broadcasted_iota(jnp.int32, (16, 128), 1), edges)
    low_mask = jnp.where(at_low == at_own, 1.0, 0.0)
    high_mask = (1.0 - low_mask).astype(jnp.bfloat16)
    low_mask = low_mask.astype(jnp.bfloat16)

    data_re = strain[0, 0, 0].astype(jnp.float32)
    data_im = strain[0, 0, 1].astype(jnp.float32)
    other_re = partner[0].astype(jnp.float32)
    other_im = partner[1].astype(jnp.float32)

    def halves(value):
        top = value.astype(jnp.bfloat16)
        return top, (value - top.astype(jnp.float32)).astype(jnp.bfloat16)

    def products(unit, h):
        for t in range(2):
            lanes = slice(t * 128, t * 128 + 128)
            slot = order[unit * UNIT + 2 * h + t]
            slot = jnp.where(slot == slots, 0, slot)
            q, m = lax.div(slot, width), lax.rem(slot, width)
            tmpl_re = blocks[q, m, 0].astype(jnp.float32)
            tmpl_im = blocks[q, m, 1].astype(jnp.float32)

            def put(at, value):
                cross[h, at : at + 16, lanes] = value

            for at, value in (
                (0, data_re * tmpl_re + data_im * tmpl_im),
                (16, data_im * tmpl_re - data_re * tmpl_im),
            ):
                top, rest = halves(value)
                put(at, top * low_mask)
                put(at + 32, top * high_mask)
                put(at + 64, rest * low_mask)
                put(at + 96, rest * high_mask)
            for at, value in (
                (128, other_re * tmpl_re + other_im * tmpl_im),
                (144, other_im * tmpl_re - other_re * tmpl_im),
            ):
                top, rest = halves(value)
                put(at, top)
                put(at + 32, rest)
            top, rest = halves(tmpl_re * tmpl_re + tmpl_im * tmpl_im)
            put(192, top * low_mask)
            put(208, top * high_mask)
            put(224, rest * low_mask)
            put(240, rest * high_mask)
        stage[h] = jnp.dot(banded[...], cross[h], preferred_element_type=jnp.float32)

    def turn(h):
        cos, sin = twist[0], twist[1]
        for t in range(2):
            lanes = slice(t * 128, t * 128 + 128)
            for band in range(BANDS + 1):
                at = 512 if band == BANDS else 32 * band
                gap = 32 if band == BANDS else 256
                part_re = stage[h, at : at + 32, lanes]
                part_im = stage[h, at + gap : at + gap + 32, lanes]
                rows = slice(32 * band, 32 * band + 32)
                turned[h, t, rows, :128] = (part_re * cos - part_im * sin).astype(jnp.bfloat16)
                turned[h, t, rows, 128:] = (part_re * sin + part_im * cos).astype(jnp.bfloat16)

    def finish(unit, h, powers):
        both = jnp.dot(
            turned[h].reshape(576, 256), second[...], preferred_element_type=jnp.float32
        )
        for t in range(2):
            power = powers[t]
            total = jnp.sum(power, axis=0, keepdims=True)
            weight = 1.0 / power
            series = both[288 * t : 288 * t + 288]
            norm = lax.rsqrt(total)
            sum_re = sum_im = spread = 0.0
            for band in range(BANDS):
                band_re = series[32 * band : 32 * band + 32, :128]
                band_im = series[32 * band : 32 * band + 32, 128:]
                sum_re = sum_re + band_re
                sum_im = sum_im + band_im
                spread = spread + (band_re * band_re + band_im * band_im) * weight[band : band + 1]
            snr_re = sum_re * norm
            snr_im = sum_im * norm
            chi_square = spread - (snr_re * snr_re + snr_im * snr_im)
            join_re = snr_re + series[256:, :128] * norm
            join_im = snr_im + series[256:, 128:] * norm
            coherent = 0.5 * (join_re * join_re + join_im * join_im)
            chi_square = jnp.maximum(chi_square, 0.0)
            result[order[unit * UNIT + 2 * h + t]] = coherent / (
                1.0 + chi_square * (1.0 / (2 * (BANDS - 1)))
            )

    for q in range(assign):
        fetch(q).wait()
    for h in range(UNIT // 2):
        products(0, h)
    done = 0
    for q in range(assign):
        last = q == assign - 1
        upto = lax.div(ends[q] + (UNIT - 1 if last else 0), UNIT)

        @pl.loop(done, upto)
        def _(unit):
            powers = []
            for h in range(UNIT // 2):
                turn(h)
                powers.append(
                    [
                        jnp.sum(stage[h, 576:584, t * 128 : t * 128 + 128], axis=1, keepdims=True) + EPS
                        for t in range(2)
                    ]
                )
            for h in range(UNIT // 2):
                finish(unit, h, powers[h])
                products(unit + 1, h)

        for g in range(q + 1):

            @pl.when((ends[g] <= UNIT * upto) & (ends[g] > UNIT * done) if not last else ends[g] > UNIT * done)
            def _(g=g):
                give(g).start()

        done = upto

    for q in range(assign):
        give(q).wait()


def correlate(held, strain, partner, bank_list, block_len, edges):
    _, owned, width, _, half_rows, bins = held.shape
    assign = bank_list.shape[1]
    slots = assign * width
    vmem = pl.BlockSpec(memory_space=pltpu.VMEM)
    smem = pl.BlockSpec(memory_space=pltpu.SMEM)
    hbm = pl.BlockSpec(memory_space=pl.ANY)
    return pl.pallas_call(
        filter_kernel,
        out_shape=jax.ShapeDtypeStruct((1, 1, slots, 2 * half_rows, bins), jnp.float32),
        in_specs=[hbm, vmem, vmem, smem, smem, smem, vmem, vmem, vmem],
        out_specs=hbm,
        scratch_shapes=[
            pltpu.VMEM((assign,) + held.shape[2:], held.dtype),
            pltpu.VMEM((ROWS, 256), jnp.bfloat16),
            pltpu.VMEM((UNIT // 2, 256, 256), jnp.bfloat16),
            pltpu.VMEM((UNIT // 2, ROWS, 256), jnp.float32),
            pltpu.VMEM((UNIT // 2, 2, 288, 256), jnp.bfloat16),
            pltpu.VMEM((slots + 1, 2 * half_rows, bins), jnp.float32),
            pltpu.SMEM((slots + 2 * UNIT,), jnp.int32),
            pltpu.SemaphoreType.DMA((assign,)),
            pltpu.SemaphoreType.DMA((assign,)),
        ],
        compiler_params=pltpu.CompilerParams(vmem_limit_bytes=60 * 2**20),
        name="filter",
    )(held, strain, partner, bank_list.T, block_len, edges, *tables())


def body(strain, bank, bank_list, block_len, band_edges):
    held, partner = move(bank, strain, lax.axis_size("det"))
    return correlate(held, strain, partner, bank_list, block_len, band_edges)


def solution(mesh):
    return jax.shard_map(
        body,
        mesh=mesh,
        in_specs=(
            P("det", "seg", None, None, None),
            P("seg", None, None, None, None),
            P(),
            P(),
            P(),
        ),
        out_specs=P("det", "seg", None, None, None),
        check_vma=False,
    )
```

```python
import functools

import jax
import jax.numpy as jnp
import numpy as np
from jax import lax
from jax.experimental import pallas as pl
from jax.experimental.pallas import tpu as pltpu
from jax.sharding import PartitionSpec as P

MESH = pl.DeviceIdType.MESH
EPS = 1e-06
ONE_SCALE = 1.62445
TWO_SCALE = 1.62475
BANDS = 8
ROWS = 592
REACH = 8
ALONG = 4
CHUNKS = 4
UNIT = 4


def tables():
    first = np.zeros((ROWS, 256))
    turn = 2 * np.pi * np.outer(np.arange(32), np.arange(16)) / 32
    cos, sin = np.cos(turn), np.sin(turn)
    from_re, from_im = (cos, sin), (-sin, cos)
    for out_part in range(2):
        both = np.concatenate([from_re[out_part], from_im[out_part]], axis=1)
        for band in range(BANDS):
            at = out_part * 256 + band * 32
            first[at : at + 32, :128] = np.tile(both, (1, 4))
        at = 512 + out_part * 32
        first[at : at + 32, 128:192] = np.tile(both, (1, 2))
    first *= ONE_SCALE
    first[576:584, 192:] = 1.0
    turn = 2 * np.pi * np.outer(np.arange(32), np.arange(128)) / 4096
    twist = np.stack([np.cos(turn), np.sin(turn)]) / (ONE_SCALE * TWO_SCALE)
    turn = 2 * np.pi * (np.outer(np.arange(128), np.arange(128)) % 128) / 128
    cos, sin = np.cos(turn), np.sin(turn)
    second = TWO_SCALE * np.block([[cos, sin], [-sin, cos]])
    return (
        jnp.asarray(first, jnp.bfloat16),
        jnp.asarray(twist, jnp.float32),
        jnp.asarray(second, jnp.bfloat16),
    )


def move_kernel(
    bank, strain, held, passing, partner, line, send_sem, recv_sem, pass_sem, own_sem, line_sem
):
    chunks = bank.shape[0]
    half = chunks // 2
    segs = lax.axis_size("seg")
    dets = lax.axis_size("det")
    seg = lax.axis_index("seg")
    det = lax.axis_index("det")
    core = lax.rem(seg, 2)
    low = lax.rem(lax.div(seg, 2), 2)
    part = 2 * low + core
    peer = seg + 1 - 2 * core
    across = seg + 2 - 4 * low
    last = dets - 1
    around = 4 * ALONG

    def wrapped(index):
        return lax.rem(index + segs, segs)

    def beside(index, by):
        return lax.div(index, around) * around + lax.rem(index + by + around, around)

    above = beside(seg, 4)
    below = beside(seg, -4)
    next_det = lax.rem(det + 1, dets)
    prev_det = lax.rem(det + dets - 1, dets)
    barrier = pltpu.get_barrier_semaphore()

    def greet(to_seg, to_det):
        pl.semaphore_signal(barrier, inc=1, device_id=(to_seg, to_det), device_id_type=MESH)

    greet(wrapped(seg + 4), det)
    greet(peer, det)
    greet(across, det)

    @pl.when(low == 0)
    def _():
        greet(across, prev_det)

    @pl.when((low == 1) & (det < last))
    def _():
        greet(across, det + 1)

    @pl.when(core == 0)
    def _():
        greet(below, det)

    @pl.when(core == 1)
    def _():
        greet(beside(wrapped(seg + 7), 4), det)

    @pl.when(part == 2)
    def _():
        greet(wrapped(seg + 3), det)
        greet(wrapped(seg + 5), det)

    pl.semaphore_wait(barrier, 5 - core + jnp.where((low == 1) | (det > 0), 1, 0))

    def copy(kind, source, k, slot, to_seg, to_det):
        return pltpu.make_async_remote_copy(
            src_ref=source,
            dst_ref=held.at[slot, k],
            send_sem=send_sem.at[kind],
            recv_sem=recv_sem.at[slot, jnp.where((slot == 1) | (slot == 3), 0, k)],
            device_id=(to_seg, to_det),
            device_id_type=MESH,
        )

    def arrived(slot, k):
        pltpu.make_async_copy(held.at[slot, k], held.at[slot, k], recv_sem.at[slot, k]).wait()

    def all_arrived(slot):
        pltpu.make_async_copy(held.at[slot], held.at[slot], recv_sem.at[slot, 0]).wait()

    def sent(kind, count):
        some = bank.at[pl.ds(0, count)]
        pltpu.make_async_copy(some, some, send_sem.at[kind]).wait()

    def up_across(kind, source, k, slot):
        if k % 2 == 0:
            copy(kind, source, k, slot, seg + 2, det).start()
        else:

            @pl.when(det > 0)
            def _():
                copy(kind, source, k, slot, seg + 2, det - 1).start()

            @pl.when(det == last)
            def _():
                copy(kind, source, k, slot, seg + 2, det).start()

    def sent_up_across(kind):
        sent(kind, half)

        @pl.when(det > 0)
        def _():
            sent(kind, half)

        @pl.when(det == last)
        def _():
            sent(kind, half)

    def own_along(k):
        copy(0, bank.at[k], k, 4, wrapped(seg - 4), det).start()

    def own_peer(k):
        copy(1, bank.at[k], k, 1, peer, det).start()

    def own_across(k):
        if k % 2 == 0:

            @pl.when(det < last)
            def _():
                copy(2, bank.at[k], k, 2, seg - 2, det + 1).start()

            @pl.when(det == 0)
            def _():
                copy(2, bank.at[k], k, 2, seg - 2, det).start()
        else:
            copy(2, bank.at[k], k, 2, seg - 2, next_det).start()

    def own_above(k):
        pltpu.make_async_remote_copy(
            src_ref=bank.at[k],
            dst_ref=passing.at[k],
            send_sem=send_sem.at[3],
            recv_sem=pass_sem.at[k],
            device_id=(above, det),
            device_id_type=MESH,
        ).start()

    def pass_above(k):
        pltpu.make_async_copy(passing.at[k], passing.at[k], pass_sem.at[k]).wait()
        copy(4, passing.at[k], k, 7, wrapped(below - 7), det).start()

    def pass_two(k):
        copy(5, held.at[2, k], k, 1 + 2 * core, peer, det).start()

    def pass_four_peer(k):
        copy(6, held.at[4, k], k, 3 + 2 * core, peer, det).start()

    def pass_four_across(k):
        @pl.when(low == 0)
        def _():
            up_across(7, held.at[4, k], k, 2)

        @pl.when(low == 1)
        def _():
            copy(7, held.at[4, k], k, 6, seg - 2, det).start()

    slot_across = 6 - 4 * low

    def pass_across_peer(k):
        copy(8, held.at[slot_across, k], k, slot_across - 1 + 2 * core, peer, det).start()

    stay = pltpu.make_async_copy(bank, held.at[0], own_sem)
    height = 2 * det + low
    hops = dets

    def along_line(way, hop):
        if way == 0:
            to_det = det + low
        else:
            to_det = det - 1 + low
        return pltpu.make_async_remote_copy(
            src_ref=strain.at[0, 0] if hop == 0 else line.at[way, hop - 1],
            dst_ref=partner if hop == hops - 1 else line.at[way, hop],
            send_sem=line_sem.at[0, way, hop],
            recv_sem=line_sem.at[1, way, hop],
            device_id=(across, to_det),
            device_id_type=MESH,
        )

    def on_line(way, hop):
        origin = height - hop if way == 0 else height + hop
        return (origin >= way * hops) & (origin < way * hops + hops)

    def pass_line(hop):
        for way in range(2):

            @pl.when(on_line(way, hop))
            def _(way=way):
                if hop > 0:
                    along_line(way, hop - 1).wait_recv()
                if hop < hops:
                    along_line(way, hop).start()

    for k in range(chunks):
        own_along(k)

        @pl.when(core == 0)
        def _():
            own_above(k)

        @pl.when(low == 1)
        def _():
            own_across(k)

    @pl.when(core == 1)
    def _():
        for k in range(chunks):
            own_peer(k)

    pass_line(0)
    stay.start()
    for step in range(chunks + 3):
        k = step
        if k < chunks:

            @pl.when(core == 0)
            def _():
                pass_above(k)

            arrived(4, k)
            if k % 2 == 0:

                @pl.when(part == 1)
                def _():
                    copy(9, held.at[4, k], k, 7, wrapped(seg - 3), det).start()

            pass_four_across(k)
            pass_four_peer(k)
        k = step - 1
        if 0 <= k < chunks:
            arrived(slot_across, k)
            if k % 2 == 1:

                @pl.when(part == 3)
                def _():
                    copy(9, held.at[2, k], k, 7, wrapped(seg - 5), det).start()

            pass_across_peer(k)

            @pl.when(low == 0)
            def _():
                arrived(2, k)
                pass_two(k)

        k = step - 2
        if 0 <= k < chunks:

            @pl.when(part == 1)
            def _():
                arrived(7, k)
                up_across(10, held.at[7, k], k, 5)

            @pl.when(part == 2)
            def _():
                arrived(7, k)
                copy(10, held.at[7, k], k, 6, peer, det).start()

        k = step - 3
        if 0 <= k < chunks:

            @pl.when(part == 3)
            def _():
                arrived(5, k)
                copy(10, held.at[5, k], k, 6, peer, det).start()

        if 1 <= step <= hops:
            pass_line(step)

    for hop in range(hops):
        for way in range(2):

            @pl.when(on_line(way, hop))
            def _(way=way, hop=hop):
                along_line(way, hop).wait_send()

    sent(0, chunks)
    sent(6, chunks)
    sent(8, chunks)

    @pl.when(core == 0)
    def _():
        sent(3, chunks)
        sent(4, chunks)

    @pl.when(core == 1)
    def _():
        sent(1, chunks)
        sent(9, half)

    @pl.when(low == 0)
    def _():
        sent(5, chunks)
        sent_up_across(7)

    @pl.when(low == 1)
    def _():
        sent(7, chunks)
        sent(2, half)
        sent(10, chunks)

        @pl.when(det < last)
        def _():
            sent(2, half)

        @pl.when(det == 0)
        def _():
            sent(2, half)

    @pl.when(part == 1)
    def _():
        sent_up_across(10)

    all_arrived(1)
    all_arrived(3)
    for k in range(chunks):

        @pl.when(part != 3)
        def _():
            arrived(5, k)

        @pl.when(low == 1)
        def _():
            arrived(6, k)

        @pl.when((part == 0) | (part == 3))
        def _():
            arrived(7, k)

    stay.wait()


def move(bank, strain, dets):
    owned, width = bank.shape[:2]
    spectrum = strain.shape[2:]
    bank = bank.reshape((CHUNKS, owned * width // CHUNKS) + bank.shape[2:])
    held, _, partner, _ = pl.pallas_call(
        move_kernel,
        out_shape=(
            jax.ShapeDtypeStruct((REACH,) + bank.shape, bank.dtype),
            jax.ShapeDtypeStruct(bank.shape, bank.dtype),
            jax.ShapeDtypeStruct(spectrum, strain.dtype),
            jax.ShapeDtypeStruct((2, dets - 1) + spectrum, strain.dtype),
        ),
        in_specs=[pl.BlockSpec(memory_space=pl.ANY)] * 2,
        out_specs=(pl.BlockSpec(memory_space=pl.ANY),) * 4,
        scratch_shapes=[
            pltpu.SemaphoreType.DMA((11,)),
            pltpu.SemaphoreType.DMA((REACH, CHUNKS)),
            pltpu.SemaphoreType.DMA((CHUNKS,)),
            pltpu.SemaphoreType.DMA,
            pltpu.SemaphoreType.DMA((2, 2, dets)),
        ],
        compiler_params=pltpu.CompilerParams(collective_id=0, has_side_effects=True),
        name="move",
    )(bank, strain)
    return held.reshape((REACH, owned, width) + bank.shape[2:]), partner


def band_at(bins, edges):
    return sum(jnp.where(bins >= edges[e], 1, 0) for e in range(BANDS - 1))


def filter_kernel(
    held, strain, partner, bank_list, block_len, edges, first, twist, second, out,
    blocks, banded, cross, stage, turned, result, order, block_sem, out_sem,
):
    segs = lax.axis_size("seg")
    seg = lax.axis_index("seg")
    assign = blocks.shape[0]
    owned = held.shape[1]
    width = blocks.shape[1]
    slots = assign * width

    def fetch(q):
        block = bank_list[q, seg]
        owner = lax.div(block, owned)
        offset = lax.rem(owner - seg + segs, segs)
        return pltpu.make_async_copy(
            held.at[offset, lax.rem(block, owned)], blocks.at[q], block_sem.at[q]
        )

    def give(q):
        rows = pl.ds(q * width, width)
        return pltpu.make_async_copy(result.at[rows], out.at[0, 0, rows], out_sem.at[q])

    for q in range(assign):
        fetch(q).start()

    ends = []
    end = 0
    for q in range(assign):
        live = block_len[bank_list[q, seg]]

        @pl.loop(0, live)
        def _(m, q=q, start=end):
            order[start + m] = q * width + m

        end = end + live
        ends.append(end)

        @pl.loop(live, width)
        def _(m, q=q):
            result[q * width + m] = jnp.zeros(result.shape[1:], jnp.float32)

    for m in range(2 * UNIT):
        order[end + m] = slots

    row = lax.broadcasted_iota(jnp.int32, (ROWS, 256), 0)
    lane = lax.broadcasted_iota(jnp.int32, (1, 256), 1)
    high_lane = jnp.where(lane < 128, lax.rem(lax.div(lane, 32), 2), lax.rem(lax.div(lane, 16), 2))
    lane_band = band_at(lax.rem(lane, 16) * 128 + 127 * high_lane, edges)
    row_band = jnp.where(row < 512, lax.rem(lax.div(row, 32), BANDS), row - 576)
    keep = ((row >= 512) & (row < 576)) | (row_band == lane_band)
    banded[...] = jnp.where(keep, first[...].astype(jnp.float32), 0.0).astype(jnp.bfloat16)

    bins = lax.broadcasted_iota(jnp.int32, (16, 128), 0) * 128
    at_low = band_at(bins, edges)
    at_own = band_at(bins + lax.broadcasted_iota(jnp.int32, (16, 128), 1), edges)
    low_mask = jnp.where(at_low == at_own, 1.0, 0.0)
    high_mask = (1.0 - low_mask).astype(jnp.bfloat16)
    low_mask = low_mask.astype(jnp.bfloat16)

    data_re = strain[0, 0, 0].astype(jnp.float32)
    data_im = strain[0, 0, 1].astype(jnp.float32)
    other_re = partner[0].astype(jnp.float32)
    other_im = partner[1].astype(jnp.float32)

    def halves(value):
        top = value.astype(jnp.bfloat16)
        return top, (value - top.astype(jnp.float32)).astype(jnp.bfloat16)

    def products(unit, h):
        for t in range(2):
            lanes = slice(t * 128, t * 128 + 128)
            slot = order[unit * UNIT + 2 * h + t]
            slot = jnp.where(slot == slots, 0, slot)
            q, m = lax.div(slot, width), lax.rem(slot, width)
            tmpl_re = blocks[q, m, 0].astype(jnp.float32)
            tmpl_im = blocks[q, m, 1].astype(jnp.float32)

            def put(at, value):
                cross[h, at : at + 16, lanes] = value

            for at, value in (
                (0, data_re * tmpl_re + data_im * tmpl_im),
                (16, data_im * tmpl_re - data_re * tmpl_im),
            ):
                top, rest = halves(value)
                put(at, top * low_mask)
                put(at + 32, top * high_mask)
                put(at + 64, rest * low_mask)
                put(at + 96, rest * high_mask)
            for at, value in (
                (128, other_re * tmpl_re + other_im * tmpl_im),
                (144, other_im * tmpl_re - other_re * tmpl_im),
            ):
                top, rest = halves(value)
                put(at, top)
                put(at + 32, rest)
            top, rest = halves(tmpl_re * tmpl_re + tmpl_im * tmpl_im)
            put(192, top * low_mask)
            put(208, top * high_mask)
            put(224, rest * low_mask)
            put(240, rest * high_mask)
        stage[h] = jnp.dot(banded[...], cross[h], preferred_element_type=jnp.float32)

    def turn(h):
        cos, sin = twist[0], twist[1]
        for t in range(2):
            lanes = slice(t * 128, t * 128 + 128)
            for band in range(BANDS + 1):
                at = 512 if band == BANDS else 32 * band
                gap = 32 if band == BANDS else 256
                part_re = stage[h, at : at + 32, lanes]
                part_im = stage[h, at + gap : at + gap + 32, lanes]
                rows = slice(32 * band, 32 * band + 32)
                turned[h, t, rows, :128] = (part_re * cos - part_im * sin).astype(jnp.bfloat16)
                turned[h, t, rows, 128:] = (part_re * sin + part_im * cos).astype(jnp.bfloat16)

    def finish(unit, h, powers):
        both = jnp.dot(
            turned[h].reshape(576, 256), second[...], preferred_element_type=jnp.float32
        )
        for t in range(2):
            power = powers[t]
            total = jnp.sum(power, axis=0, keepdims=True)
            weight = 1.0 / power
            series = both[288 * t : 288 * t + 288]
            norm = lax.rsqrt(total)
            sum_re = sum_im = spread = 0.0
            for band in range(BANDS):
                band_re = series[32 * band : 32 * band + 32, :128]
                band_im = series[32 * band : 32 * band + 32, 128:]
                sum_re = sum_re + band_re
                sum_im = sum_im + band_im
                spread = spread + (band_re * band_re + band_im * band_im) * weight[band : band + 1]
            snr_re = sum_re * norm
            snr_im = sum_im * norm
            chi_square = spread - (snr_re * snr_re + snr_im * snr_im)
            join_re = snr_re + series[256:, :128] * norm
            join_im = snr_im + series[256:, 128:] * norm
            coherent = 0.5 * (join_re * join_re + join_im * join_im)
            chi_square = jnp.maximum(chi_square, 0.0)
            result[order[unit * UNIT + 2 * h + t]] = coherent / (
                1.0 + chi_square * (1.0 / (2 * (BANDS - 1)))
            )

    for q in range(assign):
        fetch(q).wait()
    for h in range(UNIT // 2):
        products(0, h)
    done = 0
    for q in range(assign):
        last = q == assign - 1
        upto = lax.div(ends[q] + (UNIT - 1 if last else 0), UNIT)

        @pl.loop(done, upto)
        def _(unit):
            powers = []
            for h in range(UNIT // 2):
                turn(h)
                powers.append(
                    [
                        jnp.sum(stage[h, 576:584, t * 128 : t * 128 + 128], axis=1, keepdims=True) + EPS
                        for t in range(2)
                    ]
                )
            for h in range(UNIT // 2):
                finish(unit, h, powers[h])
                products(unit + 1, h)

        for g in range(q + 1):

            @pl.when((ends[g] <= UNIT * upto) & (ends[g] > UNIT * done) if not last else ends[g] > UNIT * done)
            def _(g=g):
                give(g).start()

        done = upto

    for q in range(assign):
        give(q).wait()


def correlate(held, strain, partner, bank_list, block_len, edges):
    _, owned, width, _, half_rows, bins = held.shape
    assign = bank_list.shape[1]
    slots = assign * width
    vmem = pl.BlockSpec(memory_space=pltpu.VMEM)
    smem = pl.BlockSpec(memory_space=pltpu.SMEM)
    hbm = pl.BlockSpec(memory_space=pl.ANY)
    return pl.pallas_call(
        filter_kernel,
        out_shape=jax.ShapeDtypeStruct((1, 1, slots, 2 * half_rows, bins), jnp.float32),
        in_specs=[hbm, vmem, vmem, smem, smem, smem, vmem, vmem, vmem],
        out_specs=hbm,
        scratch_shapes=[
            pltpu.VMEM((assign,) + held.shape[2:], held.dtype),
            pltpu.VMEM((ROWS, 256), jnp.bfloat16),
            pltpu.VMEM((UNIT // 2, 256, 256), jnp.bfloat16),
            pltpu.VMEM((UNIT // 2, ROWS, 256), jnp.float32),
            pltpu.VMEM((UNIT // 2, 2, 288, 256), jnp.bfloat16),
            pltpu.VMEM((slots + 1, 2 * half_rows, bins), jnp.float32),
            pltpu.SMEM((slots + 2 * UNIT,), jnp.int32),
            pltpu.SemaphoreType.DMA((assign,)),
            pltpu.SemaphoreType.DMA((assign,)),
        ],
        compiler_params=pltpu.CompilerParams(vmem_limit_bytes=60 * 2**20),
        name="filter",
    )(held, strain, partner, bank_list.T, block_len, edges, *tables())


def body(strain, bank, bank_list, block_len, band_edges):
    held, partner = move(bank, strain, lax.axis_size("det"))
    return correlate(held, strain, partner, bank_list, block_len, band_edges)


def solution(mesh):
    return jax.shard_map(
        body,
        mesh=mesh,
        in_specs=(
            P("det", "seg", None, None, None),
            P("seg", None, None, None, None),
            P(),
            P(),
            P(),
        ),
        out_specs=P("det", "seg", None, None, None),
        check_vma=False,
    )
```
